512 devices in a mesh: outer: 8 (over y), inner: 16 (over x, z_hi, core), head: 4 (over z_lo).
Axes of the slice: x: 4, y: 8, z: 8 (z_hi: 2, z_lo: 4; z = z_hi * 4 + z_lo), core: 2. Of those that a mesh axis runs over, the one named last changes fastest.
Arguments:
- queries: bfloat16 [65536, 32, 128], P(('outer', 'inner'), 'head'), may hold values from -250 to 250
- keys: bfloat16 [65536, 8, 128], P(('outer', 'inner'), 'head'), may hold values from -10 to 10
- values: bfloat16 [65536, 8, 128], P(('outer', 'inner'), 'head'), may hold values from -6 to 6
- segment_ids: int32 [65536], replicated, may hold values from 0 to 191, never falling along the last dimension, each value on 1 to 1024 neighbouring positions
Outputs:
- attended: bfloat16 [65536, 32, 128], P(('outer', 'inner'), 'head')
The draws below stay inside these ranges and needn't reach their ends.
Inputs may be any that keep to these rules, and one draw needn't show every extreme that they name: `segment_ids`: segment ids never fall; every document has 1 to 1024 tokens and one has exactly 1024.
All inputs are finite; a program needn't handle non-finite values.
Results may differ from the reference program's by a relative error of at most 0.0035.
Values may be sent and summed in bfloat16 or wider, within the bound.
A program may use at most 64 MiB of HBM per device.

```python
import math
import jax
import jax.numpy as jnp
import numpy as np
from jax import lax

QH = 32
KVH = 8
HD = 128
S_DEV = 512
TOKENS = 65536
MOST = 1024
DOCS = 192


def base_keys(key):
    return jax.random.normal(jax.random.fold_in(key, 11), (TOKENS, KVH, HD), jnp.float32)


def draw_keys(key, part):
    base = base_keys(key)
    return base.astype(jnp.bfloat16)


def draw_queries(key, part):
    key = jax.random.fold_in(key, 5)
    fresh = jax.random.normal(key, (TOKENS, QH, HD), jnp.float32)
    return fresh.astype(jnp.bfloat16)


def level_of(own_key, dims, cuts, low, top_value):
    loudness, own = 1.0, jax.random.fold_in(own_key, 6)
    for position, shards_of in cuts:
        draws = jnp.exp(jax.random.uniform(jax.random.fold_in(own, position), (shards_of,), jnp.float32, low / len(cuts), top_value / len(cuts)))
        loudness = loudness * jnp.repeat(draws, dims[position] // shards_of).reshape([-1 if axis == position else 1 for axis in range(len(dims))])
    return loudness


def split_up(count, total, most, lean):
    weights = [(1 << 20) // math.isqrt(grade ** lean) + 1 for grade in range(2, count + 1)]
    rest, holding = total - most - (count - 1), [1] * (count - 1)
    while rest > 0:
        candidates = [i for i in range(count - 1) if holding[i] < most]
        mass, left = sum([weights[i] for i in candidates]), rest
        for i in candidates:
            more = min(most - holding[i], max(1, left * weights[i] // mass), rest)
            holding[i] = holding[i] + more
            rest = rest - more
    return np.array([most] + holding)


def uneven_parts(key, amount, total, most, skew):
    if amount == 2:
        one = jax.random.randint(key, (), max(1, total - most), min(most, total - 1) + 1)
        return jnp.stack([one, total - one])
    sizes = jnp.asarray(split_up(amount, total, most, skew), jnp.int32)
    pairs = (amount - 1) // 2
    source_of, receiver = sizes[1:1 + 2 * pairs:2], sizes[2:2 + 2 * pairs:2]
    margin = jnp.minimum(source_of - 1, most - receiver)
    shifted = jax.random.randint(jax.random.fold_in(key, 1), (pairs,), 0, 1 << 20) % (margin + 1)
    sizes = sizes.at[1:1 + 2 * pairs:2].set(source_of - shifted).at[2:2 + 2 * pairs:2].set(receiver + shifted)
    return sizes[jax.random.permutation(jax.random.fold_in(key, 2), amount)]


def gaussian(key, dims, scale, bound, shards=(), held_as=jnp.bfloat16):
    drawn = scale * jax.random.normal(key, dims, jnp.float32)
    if shards:
        drawn = drawn * level_of(key, dims, shards, -0.22, 0.18)
    return jnp.clip(drawn, -bound, bound).astype(held_as)


def setup_inputs(seed: int = 0) -> dict:
    streams_of = jax.random.split(jax.random.key(seed), 5)
    queries = draw_queries(jax.random.fold_in(streams_of[4], 71), 0)
    keys = draw_keys(jax.random.fold_in(streams_of[4], 71), 0)
    values = gaussian(streams_of[2], (TOKENS, KVH, HD), 1.0, 6.0, ((0, 128), (1, 4)))
    segment_ids = jnp.searchsorted(jnp.cumsum(uneven_parts(streams_of[3], DOCS, TOKENS, MOST, 2)), jnp.arange(TOKENS), side="right").astype(jnp.int32)
    return {"queries": queries, "keys": keys, "values": values, "segment_ids": segment_ids}


def attend(block_q, block_k, block_v, allowed):
    rows, heads, width = block_q.shape
    kv_heads = block_k.shape[1]
    group = heads // kv_heads
    grouped = block_q.reshape(rows, kv_heads, group, width)
    scale = width ** -0.5

    def one_head(index):
        query_h = lax.dynamic_index_in_dim(grouped, index, 1, False).astype(jnp.float32)
        key_h = lax.dynamic_index_in_dim(block_k, index, 1, False).astype(jnp.float32)
        value_h = lax.dynamic_index_in_dim(block_v, index, 1, False)
        scores = jnp.einsum("sgd,td->gst", query_h, key_h) * scale
        scores = jnp.where(allowed[None], scores, -1e30)
        top = jnp.max(scores, axis=-1, keepdims=True)
        weights = jnp.exp(scores - top)
        total = jnp.sum(weights, axis=-1)
        rounded = weights.astype(jnp.bfloat16).astype(jnp.float32)
        mixed = jnp.einsum("gst,td->gsd", rounded, value_h.astype(jnp.float32))
        return (mixed / total[..., None]).astype(jnp.bfloat16)

    heads_out = lax.map(one_head, jnp.arange(kv_heads, dtype=jnp.int32))
    return heads_out.transpose(2, 0, 1, 3).reshape(rows, heads, width)


def reference(queries, keys, values, segment_ids):
    front = 2 * S_DEV
    padded_k = jnp.concatenate([jnp.zeros((front,) + keys.shape[1:], keys.dtype), keys], axis=0)
    padded_v = jnp.concatenate([jnp.zeros((front,) + values.shape[1:], values.dtype), values], axis=0)
    padded_s = jnp.concatenate([jnp.full((front,), -1, jnp.int32), segment_ids], axis=0)

    def one_block(block):
        start = (block * S_DEV).astype(jnp.int32)
        block_q = lax.dynamic_slice_in_dim(queries, start, S_DEV, 0)
        block_k = lax.dynamic_slice_in_dim(padded_k, start, 3 * S_DEV, 0)
        block_v = lax.dynamic_slice_in_dim(padded_v, start, 3 * S_DEV, 0)
        seg_k = lax.dynamic_slice_in_dim(padded_s, start, 3 * S_DEV, 0)
        seg_q = lax.dynamic_slice_in_dim(segment_ids, start, S_DEV, 0)
        query_pos = jnp.arange(S_DEV, dtype=jnp.int32) + 2 * S_DEV
        key_pos = jnp.arange(3 * S_DEV, dtype=jnp.int32)
        allowed = (seg_k[None, :] == seg_q[:, None]) & (key_pos[None, :] <= query_pos[:, None])
        return attend(block_q, block_k, block_v, allowed)

    blocks = lax.map(one_block, jnp.arange(TOKENS // S_DEV, dtype=jnp.int32))
    return blocks.reshape(TOKENS, QH, HD)
```

```python
import functools

import jax
import jax.numpy as jnp
from jax import lax
from jax.experimental import pallas as pl
from jax.experimental.pallas import tpu as pltpu
from jax.sharding import PartitionSpec as P

MESH = pl.DeviceIdType.MESH
BIG = -1e30
LOG2E = 1.4426950408889634
KEYS = 256
TILE = 512


def kernel(dims, q_hbm, k_hbm, v_hbm, s_hbm, o_hbm, q_in, q_aug, own, near, far, seg, seg_q,
           perm, k_aug, v_cat, top, total, acc, out, in_sem, out_sem, send_far, recv_far, send_near, recv_near):
    inner_size, outer_size, rows, width = dims
    chips_in = inner_size // 2
    outer, inner, head = lax.axis_index("outer"), lax.axis_index("inner"), lax.axis_index("head")
    chip, core = outer * chips_in + inner // 2, lax.rem(inner, 2)
    last_chip = outer_size * chips_in - 1
    heads = q_in.shape[0] // rows
    c = (width ** -0.5) * LOG2E
    chunks = rows // KEYS

    def chip_dev(index):
        return (index // chips_in, lax.rem(index, chips_in) * 2 + core, head)

    after, before = chip_dev(chip + 1), chip_dev(chip - 1)
    sibling = (outer, inner + 1 - 2 * core, head)
    has_before, has_after = chip > 0, chip < last_chip

    barrier = pltpu.get_barrier_semaphore()
    pl.semaphore_signal(barrier, inc=1, device_id=sibling, device_id_type=MESH)

    @pl.when(has_before)
    def _():
        pl.semaphore_signal(barrier, inc=1, device_id=before, device_id_type=MESH)

    loads = [
        pltpu.make_async_copy(k_hbm, own.at[0], in_sem.at[0]),
        pltpu.make_async_copy(v_hbm, own.at[1], in_sem.at[1]),
        pltpu.make_async_copy(q_hbm, q_in, in_sem.at[2]),
        pltpu.make_async_copy(s_hbm.at[pl.ds(pl.multiple_of(jnp.maximum(chip - 1, 0) * 8, 8), 16)], seg, in_sem.at[3]),
    ]
    for load in loads:
        load.start()

    pl.semaphore_wait(barrier, 1 + has_after.astype(jnp.int32))

    def part(ref, chunk):
        return ref.at[pl.ds(chunk * KEYS * 2, KEYS * 2)]

    def to_far(chunk, kv):
        return pltpu.make_async_remote_copy(
            src_ref=part((k_hbm, v_hbm)[kv], chunk), dst_ref=part(far.at[kv], chunk),
            send_sem=send_far.at[chunk, kv], recv_sem=recv_far.at[chunk, kv],
            device_id=after, device_id_type=MESH)

    def to_near(chunk, kv, forward):
        source = far.at[kv] if forward else (k_hbm, v_hbm)[kv]
        return pltpu.make_async_remote_copy(
            src_ref=part(source, chunk), dst_ref=part(near.at[kv], chunk),
            send_sem=send_near.at[chunk, kv], recv_sem=recv_near.at[chunk, kv],
            device_id=sibling, device_id_type=MESH)

    order = list(reversed(range(chunks)))

    @pl.when(has_after)
    def _():
        for chunk in order:
            for kv in range(2):
                to_far(chunk, kv).start()

    @pl.when(core == 0)
    def _():
        for chunk in order:
            for kv in range(2):
                to_near(chunk, kv, False).start()

    for load in loads:
        load.wait()
    at = lax.broadcasted_iota(jnp.int32, perm.shape, 0)
    source = jnp.where(at < 128, 2 * at, 2 * at - 255)
    perm[...] = (source == lax.broadcasted_iota(jnp.int32, perm.shape, 1)).astype(jnp.float32).astype(jnp.bfloat16)
    base = jnp.maximum(chip - 1, 0) * 2
    block = chip * 2 + core - base

    @pl.loop(0, rows // 128)
    def _(tile):
        span = pl.ds(pl.multiple_of(tile * 128 * heads, 128 * heads), 128 * heads)
        shape = (128 * heads, 128)
        row = lax.broadcasted_iota(jnp.int32, shape, 0)
        q = q_in[span, :].astype(jnp.float32)
        first_half = lax.rem(row, heads) < heads // 2
        q_aug[span, 0:128] = jnp.where(first_half, q, 0.0).astype(jnp.bfloat16)
        q_aug[span, 128:256] = jnp.where(first_half, 0.0, q).astype(jnp.bfloat16)
        ids = seg[pl.ds(block * 4 + tile, 1), :].astype(jnp.float32)
        picked = jnp.where(row // heads == lax.broadcasted_iota(jnp.int32, shape, 1), ids, 0.0)
        seg_q[span, :] = jnp.dot(
            picked.astype(jnp.bfloat16), jnp.ones((128, 128), jnp.bfloat16), preferred_element_type=jnp.float32)

    def process(kv_ref, key_block, chunk, first_token, last_token, own_chunk=False, init=False):
        for half in range(KEYS // 128):
            for kv, into in ((0, k_aug), (1, v_cat)):
                raw = kv_ref[kv, pl.ds(chunk * KEYS * 2 + half * 256, 256), :]
                parted = jnp.dot(perm[...], raw, preferred_element_type=jnp.float32).astype(jnp.bfloat16)
                into[half * 128:half * 128 + 128, 0:128] = parted[:128]
                into[half * 128:half * 128 + 128, 128:256] = parted[128:]
        ids = jnp.concatenate(
            [seg[pl.ds(key_block * 4 + chunk * (KEYS // 128) + i, 1), :] for i in range(KEYS // 128)],
            axis=1).astype(jnp.float32)

        @pl.loop(first_token * heads // TILE, last_token * heads // TILE)
        def _(step):
            start = pl.multiple_of(step * TILE, TILE)
            span = pl.ds(start, TILE)
            scores = lax.dot_general(
                q_aug[span, :], k_aug[...], (((1,), (1,)), ((), ())), preferred_element_type=jnp.float32)
            mine = seg_q[span, :]
            allowed = jnp.concatenate([mine] * (KEYS // 128), axis=1) == ids
            if own_chunk:
                row = lax.broadcasted_iota(jnp.int32, scores.shape, 0)
                key = lax.broadcasted_iota(jnp.int32, scores.shape, 1)
                allowed = allowed & (row - heads * key >= heads * chunk * KEYS - start)
            scores = jnp.where(allowed, scores, BIG)
            peak = jnp.max(scores, axis=1, keepdims=True)
            if init:
                new_top = jnp.broadcast_to(peak, (TILE, 128))
            else:
                old_top = top[span, :]
                new_top = jnp.maximum(old_top, peak)
            weights = jnp.exp2((scores - jnp.concatenate([new_top] * (KEYS // 128), axis=1)) * c)
            added = jnp.sum(weights, axis=1, keepdims=True)
            mixed = jnp.dot(weights.astype(jnp.bfloat16), v_cat[...], preferred_element_type=jnp.float32)
            first_half = lax.rem(lax.broadcasted_iota(jnp.int32, (TILE, 128), 0), heads) < heads // 2
            mixed = jnp.where(first_half, mixed[:, :128], mixed[:, 128:])
            top[span, :] = new_top
            if init:
                total[span, :] = jnp.broadcast_to(added, (TILE, 128))
                acc[span, :] = mixed
            else:
                fade = jnp.exp2((old_top - new_top) * c)
                total[span, :] = total[span, :] * fade + added
                acc[span, :] = acc[span, :] * fade + mixed

    def finish(first_token, last_token, index):
        @pl.loop(first_token * heads // TILE, last_token * heads // TILE)
        def _(step):
            span = pl.ds(pl.multiple_of(step * TILE, TILE), TILE)
            out[span, :] = (acc[span, :] / total[span, :]).astype(jnp.bfloat16)

        span = pl.ds(first_token * heads, (last_token - first_token) * heads)
        copy = pltpu.make_async_copy(out.at[span], o_hbm.at[span], out_sem.at[index])
        copy.start()
        return copy

    for chunk in range(chunks):
        process(own, block, chunk, chunk * KEYS, rows, own_chunk=True, init=chunk == 0)

    @pl.when(core == 1)
    def _():
        for chunk in order:
            for kv in range(2):
                to_near(chunk, kv, False).wait_recv()
            process(near, block - 1, chunk, 0, rows)

    for chunk in order:
        last = chunk == 0

        @pl.when(has_before)
        def _():
            for kv in range(2):
                to_far(chunk, kv).wait_recv()

        @pl.when(has_before & (core == 1))
        def _():
            for kv in range(2):
                to_near(chunk, kv, True).start()

        if not last:
            @pl.when(has_before)
            def _():
                process(far, block - 2, chunk, 0, (chunk + 1) * KEYS)

        @pl.when(has_before & (core == 0))
        def _():
            for kv in range(2):
                to_near(chunk, kv, True).wait_recv()
            process(near, block - 1, chunk, 0, rows)

        if last:
            second = finish((chunk + 1) * KEYS, rows, 1)

            @pl.when(has_before)
            def _():
                process(far, block - 2, chunk, 0, (chunk + 1) * KEYS)

            first = finish(0, (chunk + 1) * KEYS, 0)

    @pl.when(has_after)
    def _():
        for chunk in order:
            for kv in range(2):
                to_far(chunk, kv).wait_send()

    @pl.when((core == 0) | has_before)
    def _():
        for chunk in order:
            for kv in range(2):
                to_near(chunk, kv, False).wait_send()

    first.wait()
    second.wait()


def shards(queries, keys, values, segment_ids):
    rows, heads, width = queries.shape
    kv_heads = keys.shape[1]
    dims = (lax.axis_size("inner"), lax.axis_size("outer"), rows, width)
    any_space = pl.BlockSpec(memory_space=pl.ANY)
    kv = lambda: pltpu.VMEM((2, rows * kv_heads, width), jnp.bfloat16)
    wide = lambda: pltpu.VMEM((rows * heads, width), jnp.float32)
    chunk_sems = lambda: pltpu.SemaphoreType.DMA((rows // KEYS, 2))
    result = pl.pallas_call(
        functools.partial(kernel, dims),
        out_shape=jax.ShapeDtypeStruct((rows * heads, width), jnp.bfloat16),
        in_specs=[any_space] * 4,
        out_specs=any_space,
        scratch_shapes=[
            pltpu.VMEM((rows * heads, width), jnp.bfloat16),
            pltpu.VMEM((rows * heads, 2 * width), jnp.bfloat16),
            kv(), kv(), kv(),
            pltpu.VMEM((16, 128), jnp.int32),
            wide(),
            pltpu.VMEM((256, 256), jnp.bfloat16),
            pltpu.VMEM((KEYS, 2 * width), jnp.bfloat16),
            pltpu.VMEM((KEYS, 2 * width), jnp.bfloat16),
            wide(), wide(), wide(),
            pltpu.VMEM((rows * heads, width), jnp.bfloat16),
            pltpu.SemaphoreType.DMA((4,)),
            pltpu.SemaphoreType.DMA((2,)),
            chunk_sems(), chunk_sems(), chunk_sems(), chunk_sems(),
        ],
        compiler_params=pltpu.CompilerParams(
            collective_id=0, has_side_effects=True, vmem_limit_bytes=62 * 1024 * 1024),
    )(
        queries.reshape(rows * heads, width),
        keys.reshape(rows * kv_heads, width),
        values.reshape(rows * kv_heads, width),
        segment_ids.reshape(-1, 128),
    )
    return result.reshape(rows, heads, width)


def solution(mesh):
    return jax.shard_map(
        shards,
        mesh=mesh,
        in_specs=(
            P(("outer", "inner"), "head", None),
            P(("outer", "inner"), "head", None),
            P(("outer", "inner"), "head", None),
            P(),
        ),
        out_specs=P(("outer", "inner"), "head", None),
        check_vma=False,
    )
```

```python
import functools

import jax
import jax.numpy as jnp
from jax import lax
from jax.experimental import pallas as pl
from jax.experimental.pallas import tpu as pltpu
from jax.sharding import PartitionSpec as P

MESH = pl.DeviceIdType.MESH
BIG = -1e30
LOG2E = 1.4426950408889634
LANES = 128


def kernel(dims, q_hbm, k_hbm, v_hbm, s_hbm, o_hbm, q_in, q_aug, own, near, far, relay, seg, seg_q,
           perm, k_t, v_cat, top, total, acc, out, in_sem, out_sem,
           send_sem, pass_sem, recv_near, recv_far, relay_send, relay_recv):
    inner_size, outer_size, rows, width = dims
    chips_in = inner_size // 2
    outer, inner, head = lax.axis_index("outer"), lax.axis_index("inner"), lax.axis_index("head")
    chip, core = outer * chips_in + inner // 2, lax.rem(inner, 2)
    early = lax.rem(chip, 2) == 0
    has_before, has_after = chip > 0, chip < outer_size * chips_in - 1
    heads = q_in.shape[0] // rows
    kv_rows = own.shape[1] // rows * LANES
    c = (width ** -0.5) * LOG2E

    def device(index, which):
        return (index // chips_in, lax.rem(index, chips_in) * 2 + which, head)

    sibling = (outer, inner + 1 - 2 * core, head)

    barrier = pltpu.get_barrier_semaphore()
    pl.semaphore_signal(barrier, inc=1, device_id=sibling, device_id_type=MESH)

    @pl.when(has_before)
    def _():
        pl.semaphore_signal(barrier, inc=1, device_id=device(chip - 1, 1), device_id_type=MESH)

    @pl.when(has_before & (core == 0))
    def _():
        pl.semaphore_signal(barrier, inc=1, device_id=device(chip - 1, 0), device_id_type=MESH)

    loads = [
        pltpu.make_async_copy(k_hbm, own.at[0], in_sem.at[0]),
        pltpu.make_async_copy(v_hbm, own.at[1], in_sem.at[1]),
        pltpu.make_async_copy(q_hbm, q_in, in_sem.at[2]),
        pltpu.make_async_copy(s_hbm.at[pl.ds(pl.multiple_of(jnp.maximum(chip - 1, 0) * 8, 8), 16)], seg, in_sem.at[3]),
    ]

    def piece(ref, tile):
        return ref.at[pl.ds(tile * kv_rows, kv_rows)]

    def copies(source, target, tile, send, recv, to, slot=0):
        return [
            pltpu.make_async_remote_copy(
                src_ref=piece(source[kv], tile), dst_ref=piece(target.at[kv], tile),
                send_sem=send.at[slot + tile, kv], recv_sem=recv.at[tile, kv], device_id=to, device_id_type=MESH)
            for kv in range(2)]

    mine = (k_hbm, v_hbm)
    near_parts, far_parts, relay_parts = ([ref.at[kv] for kv in range(2)] for ref in (near, far, relay))

    def second_by_1(tile):
        return copies(mine, far, tile, send_sem, recv_far, device(chip + 1, 1))

    def first_by_1(tile):
        return copies(near_parts, far, tile, send_sem, recv_far, device(chip + 1, 0), 4)

    def second_by_0(tile):
        return copies(relay_parts, near, tile, send_sem, recv_near, device(chip + 1, 0))

    def first_by_0(tile):
        return copies(mine, far, tile, send_sem, recv_far, device(chip + 1, 0), 4)

    def to_core_1(tile):
        return copies(mine, near, tile, pass_sem, recv_near, sibling)

    def to_relay(tile):
        return copies(mine, relay, tile, relay_send, relay_recv, sibling)

    def pass_to_0(tile):
        return copies(far_parts, near, tile, pass_sem, recv_near, sibling)

    def pass_to_1(tile):
        return copies(near_parts, far, tile, relay_send, recv_far, sibling)

    def start(pair):
        for copy in pair:
            copy.start()

    def wait_recv(pair):
        for copy in pair:
            copy.wait_recv()

    def wait_send(pair):
        for copy in pair:
            copy.wait_send()

    def send():
        pl.semaphore_wait(barrier, 1 + has_after.astype(jnp.int32) * (1 + core))

        @pl.when(core == 1)
        def _():
            @pl.when(has_after)
            def _():
                start(second_by_1(3))
                start(to_relay(1))
                start(to_relay(0))
                start(second_by_1(2))
            wait_recv(to_core_1(3))
            wait_recv(to_core_1(1))

            @pl.when(has_after)
            def _():
                start(first_by_1(3))
                start(first_by_1(1))

        @pl.when(core == 0)
        def _():
            for tile in (3, 1, 2, 0):
                start(to_core_1(tile))

            @pl.when(has_after)
            def _():
                for tile in (1, 0):
                    wait_recv(to_relay(tile))
                    start(second_by_0(tile))
                start(first_by_0(2))
                start(first_by_0(0))

    for load in loads:
        load.start()

    @pl.when(jnp.logical_not(early))
    def _():
        send()

    at = lax.broadcasted_iota(jnp.int32, perm.shape, 0)
    taken = jnp.where(at < LANES, 2 * at, 2 * at - 2 * LANES + 1)
    perm[...] = (taken == lax.broadcasted_iota(jnp.int32, perm.shape, 1)).astype(jnp.float32).astype(jnp.bfloat16)
    for load in loads:
        load.wait()
    base = jnp.maximum(chip - 1, 0) * 2
    block = chip * 2 + core - base

    shape = (LANES * heads, LANES)
    row = lax.broadcasted_iota(jnp.int32, shape, 0)
    first_half = lax.rem(row, heads) < heads // 2
    for tile in range(rows // LANES):
        span = pl.ds(tile * LANES * heads, LANES * heads)
        q = q_in[span, :].astype(jnp.float32)
        q_aug[span, 0:width] = jnp.where(first_half, q, 0.0).astype(jnp.bfloat16)
        q_aug[span, width:2 * width] = jnp.where(first_half, 0.0, q).astype(jnp.bfloat16)
        ids = seg[pl.ds(block * 4 + tile, 1), :].astype(jnp.float32)
        picked = jnp.where(row // heads == lax.broadcasted_iota(jnp.int32, shape, 1), ids, 0.0)
        seg_q[span, :] = jnp.dot(
            picked.astype(jnp.bfloat16), jnp.ones((LANES, LANES), jnp.bfloat16), preferred_element_type=jnp.float32)

    def process(kv_ref, key_block, tiles, first_token, last_token, own_keys=False, init=False):
        for part, tile in enumerate(tiles):
            span = pl.ds(part * LANES, LANES)
            parted = [
                jnp.dot(perm[...], kv_ref[kv, pl.ds(tile * kv_rows, kv_rows), :], preferred_element_type=jnp.float32)
                for kv in range(2)]
            k_t[0:width, span] = parted[0][:LANES].T.astype(jnp.bfloat16)
            k_t[width:2 * width, span] = parted[0][LANES:].T.astype(jnp.bfloat16)
            v_cat[span, 0:width] = parted[1][:LANES].astype(jnp.bfloat16)
            v_cat[span, width:2 * width] = parted[1][LANES:].astype(jnp.bfloat16)
        ids = jnp.concatenate(
            [seg[pl.ds(key_block * 4 + tile, 1), :] for tile in tiles], axis=1).astype(jnp.float32)

        begin, count = first_token * heads, (last_token - first_token) * heads
        span = pl.ds(begin, count)
        scores = jnp.dot(q_aug[span, :], k_t[...], preferred_element_type=jnp.float32)
        allowed = jnp.concatenate([seg_q[span, :]] * len(tiles), axis=1) == ids
        if own_keys:
            line = lax.broadcasted_iota(jnp.int32, scores.shape, 0)
            key = lax.broadcasted_iota(jnp.int32, scores.shape, 1)
            allowed = allowed & (line - heads * key >= heads * tiles[0] * LANES - begin)
        scores = jnp.where(allowed, scores, BIG)
        peak = jnp.max(scores, axis=1, keepdims=True)
        if init:
            new_top = jnp.broadcast_to(peak, (count, LANES))
        else:
            old_top = top[span, :]
            new_top = jnp.maximum(old_top, peak)
        weights = jnp.exp2((scores - jnp.concatenate([new_top] * len(tiles), axis=1)) * c)
        added = weights[:, :LANES] + weights[:, LANES:]
        mixed = jnp.dot(weights.astype(jnp.bfloat16), v_cat[...], preferred_element_type=jnp.float32)
        line = lax.broadcasted_iota(jnp.int32, (count, width), 0)
        mixed = jnp.where(lax.rem(line, heads) < heads // 2, mixed[:, :width], mixed[:, width:])
        top[span, :] = new_top
        if init:
            total[span, :] = added
            acc[span, :] = mixed
        else:
            fade = jnp.exp2((old_top - new_top) * c)
            total[span, :] = total[span, :] * fade + added
            acc[span, :] = acc[span, :] * fade + mixed

    def finish(first_token, last_token, index):
        span = pl.ds(first_token * heads, (last_token - first_token) * heads)
        out[span, :] = (acc[span, :] / jnp.sum(total[span, :], axis=1, keepdims=True)).astype(jnp.bfloat16)
        copy = pltpu.make_async_copy(out.at[span], o_hbm.at[span], out_sem.at[index])
        copy.start()
        return copy

    half = rows // 2
    process(own, block, (0, 1), 0, rows, own_keys=True, init=True)
    process(own, block, (2, 3), half, rows, own_keys=True)

    @pl.when(early)
    def _():
        send()

    near_there = has_before | (core == 1)
    for group, (direct, passed) in enumerate(((1, 3), (0, 2))):
        @pl.when(has_before & (core == 0))
        def _():
            wait_recv(second_by_0(direct))
            start(pass_to_1(direct))
            wait_recv(pass_to_0(passed))

        if group == 1:
            @pl.when(core == 1)
            def _():
                wait_recv(to_core_1(2))
                wait_recv(to_core_1(0))

        @pl.when(near_there)
        def _():
            process(near, block - 1, (direct, passed), 0, rows)

    @pl.when(has_before & (core == 1))
    def _():
        for tile in (3, 2):
            wait_recv(second_by_1(tile))
            start(pass_to_0(tile))

    @pl.when(has_before & (core == 0))
    def _():
        wait_recv(first_by_1(3))
        wait_recv(first_by_0(2))

    @pl.when(has_before)
    def _():
        process(far, block - 2, (2, 3), 0, rows)

    late = finish(half, rows, 1)

    @pl.when(has_before & (core == 1))
    def _():
        wait_recv(pass_to_1(1))
        wait_recv(pass_to_1(0))

    @pl.when(has_before & (core == 0))
    def _():
        wait_recv(first_by_1(1))
        wait_recv(first_by_0(0))

    @pl.when(has_before)
    def _():
        process(far, block - 2, (0, 1), 0, half)

    soon = finish(0, half, 0)

    @pl.when(has_after & (core == 1))
    def _():
        for pair in (second_by_1(3), second_by_1(2), to_relay(1), to_relay(0), first_by_1(3), first_by_1(1)):
            wait_send(pair)

    @pl.when(has_before & (core == 1))
    def _():
        for pair in (pass_to_0(3), pass_to_0(2)):
            wait_send(pair)

    @pl.when(core == 0)
    def _():
        for tile in (3, 1, 2, 0):
            wait_send(to_core_1(tile))

    @pl.when(has_after & (core == 0))
    def _():
        for pair in (second_by_0(1), second_by_0(0), first_by_0(2), first_by_0(0)):
            wait_send(pair)

    @pl.when(has_before & (core == 0))
    def _():
        for pair in (pass_to_1(1), pass_to_1(0)):
            wait_send(pair)

    late.wait()
    soon.wait()


def shards(queries, keys, values, segment_ids):
    rows, heads, width = queries.shape
    kv_heads = keys.shape[1]
    dims = (lax.axis_size("inner"), lax.axis_size("outer"), rows, width)
    in_hbm = pl.BlockSpec(memory_space=pltpu.HBM)
    kv = lambda parts=1: pltpu.VMEM((2, rows * kv_heads // parts, width), jnp.bfloat16)
    wide = lambda: pltpu.VMEM((rows * heads, width), jnp.float32)
    sems = lambda count: pltpu.SemaphoreType.DMA((count, 2))
    result = pl.pallas_call(
        functools.partial(kernel, dims),
        out_shape=jax.ShapeDtypeStruct((rows * heads, width), jnp.bfloat16),
        in_specs=[in_hbm] * 4,
        out_specs=pl.BlockSpec(memory_space=pl.ANY),
        scratch_shapes=[
            pltpu.VMEM((rows * heads, width), jnp.bfloat16),
            pltpu.VMEM((rows * heads, 2 * width), jnp.bfloat16),
            kv(), kv(), kv(), kv(2),
            pltpu.VMEM((16, LANES), jnp.int32),
            wide(),
            pltpu.VMEM((2 * LANES, 2 * LANES), jnp.bfloat16),
            pltpu.VMEM((2 * width, 2 * LANES), jnp.bfloat16),
            pltpu.VMEM((2 * LANES, 2 * width), jnp.bfloat16),
            wide(), wide(), wide(),
            pltpu.VMEM((rows * heads, width), jnp.bfloat16),
            pltpu.SemaphoreType.DMA((4,)),
            pltpu.SemaphoreType.DMA((2,)),
            sems(8), sems(4), sems(4), sems(4), sems(2), sems(2),
        ],
        compiler_params=pltpu.CompilerParams(
            collective_id=0, has_side_effects=True, vmem_limit_bytes=62 * 1024 * 1024),
    )(
        queries.reshape(rows * heads, width),
        keys.reshape(rows * kv_heads, width),
        values.reshape(rows * kv_heads, width),
        segment_ids.reshape(-1, LANES),
    )
    return result.reshape(rows, heads, width)


def solution(mesh):
    return jax.shard_map(
        shards,
        mesh=mesh,
        in_specs=(
            P(("outer", "inner"), "head", None),
            P(("outer", "inner"), "head", None),
            P(("outer", "inner"), "head", None),
            P(),
        ),
        out_specs=P(("outer", "inner"), "head", None),
        check_vma=False,
    )
```

```python
import functools

import jax
import jax.numpy as jnp
from jax import lax
from jax.experimental import pallas as pl
from jax.experimental.pallas import tpu as pltpu
from jax.sharding import PartitionSpec as P

MESH = pl.DeviceIdType.MESH
BIG = -1e30
LOG2E = 1.4426950408889634
LANES = 128


def kernel(dims, q_hbm, k_hbm, v_hbm, s_hbm, out, q_in, q_aug, own, near, far, relay, seg, seg_q,
           perm, k_t, v_cat, top, total, acc, in_sem,
           send_sem, pass_sem, recv_near, recv_far, relay_send, relay_recv):
    inner_size, outer_size, rows, width = dims
    chips_in = inner_size // 2
    outer, inner, head = lax.axis_index("outer"), lax.axis_index("inner"), lax.axis_index("head")
    chip, core = outer * chips_in + inner // 2, lax.rem(inner, 2)
    early = lax.rem(chip, 2) == 0
    has_before, has_after = chip > 0, chip < outer_size * chips_in - 1
    heads = q_in.shape[0] // rows
    kv_rows = own.shape[1] // rows * LANES
    c = (width ** -0.5) * LOG2E

    def device(index, which):
        return (index // chips_in, lax.rem(index, chips_in) * 2 + which, head)

    sibling = (outer, inner + 1 - 2 * core, head)

    barrier = pltpu.get_barrier_semaphore()
    pl.semaphore_signal(barrier, inc=1, device_id=sibling, device_id_type=MESH)

    @pl.when(has_before)
    def _():
        pl.semaphore_signal(barrier, inc=1, device_id=device(chip - 1, 1), device_id_type=MESH)

    @pl.when(has_before & (core == 0))
    def _():
        pl.semaphore_signal(barrier, inc=1, device_id=device(chip - 1, 0), device_id_type=MESH)

    loads = [
        pltpu.make_async_copy(k_hbm, own.at[0], in_sem.at[0]),
        pltpu.make_async_copy(v_hbm, own.at[1], in_sem.at[1]),
        pltpu.make_async_copy(q_hbm, q_in, in_sem.at[2]),
        pltpu.make_async_copy(s_hbm.at[pl.ds(pl.multiple_of(jnp.maximum(chip - 1, 0) * 8, 8), 16)], seg, in_sem.at[3]),
    ]

    def piece(ref, tile):
        return ref.at[pl.ds(tile * kv_rows, kv_rows)]

    def copies(source, target, tile, send, recv, to, slot=0):
        return [
            pltpu.make_async_remote_copy(
                src_ref=piece(source[kv], tile), dst_ref=piece(target.at[kv], tile),
                send_sem=send.at[slot + tile, kv], recv_sem=recv.at[tile, kv], device_id=to, device_id_type=MESH)
            for kv in range(2)]

    mine = (k_hbm, v_hbm)
    near_parts, far_parts, relay_parts = ([ref.at[kv] for kv in range(2)] for ref in (near, far, relay))

    def second_by_1(tile):
        return copies(mine, far, tile, send_sem, recv_far, device(chip + 1, 1))

    def first_by_1(tile):
        return copies(near_parts, far, tile, send_sem, recv_far, device(chip + 1, 0), 4)

    def second_by_0(tile):
        return copies(relay_parts, near, tile, send_sem, recv_near, device(chip + 1, 0))

    def first_by_0(tile):
        return copies(mine, far, tile, send_sem, recv_far, device(chip + 1, 0), 4)

    def to_core_1(tile):
        return copies(mine, near, tile, pass_sem, recv_near, sibling)

    def to_relay(tile):
        return copies(mine, relay, tile, relay_send, relay_recv, sibling)

    def pass_to_0(tile):
        return copies(far_parts, near, tile, pass_sem, recv_near, sibling)

    def pass_to_1(tile):
        return copies(near_parts, far, tile, relay_send, recv_far, sibling)

    def start(pair):
        for copy in pair:
            copy.start()

    def wait_recv(pair):
        for copy in pair:
            copy.wait_recv()

    def wait_for(target, recv, tile, kv):
        pltpu.make_async_remote_copy(
            src_ref=piece(mine[kv], tile), dst_ref=piece(target.at[kv], tile), send_sem=send_sem.at[tile, kv],
            recv_sem=recv.at[tile, kv], device_id=sibling, device_id_type=MESH).wait_recv()

    def wait_send(pair):
        for copy in pair:
            copy.wait_send()

    def send():
        pl.semaphore_wait(barrier, 1 + has_after.astype(jnp.int32) * (1 + core))

        @pl.when(core == 1)
        def _():
            @pl.when(has_after)
            def _():
                start(second_by_1(3))
                start(to_relay(1))
                start(to_relay(0))
                start(second_by_1(2))
            wait_recv(to_core_1(3))
            wait_recv(to_core_1(1))

            @pl.when(has_after)
            def _():
                start(first_by_1(3))
                start(first_by_1(1))

        @pl.when(core == 0)
        def _():
            for tile in (3, 1, 2, 0):
                start(to_core_1(tile))

            @pl.when(has_after)
            def _():
                for tile in (1, 0):
                    wait_recv(to_relay(tile))
                    start(second_by_0(tile))
                start(first_by_0(2))
                start(first_by_0(0))

    for load in loads:
        load.start()

    @pl.when(jnp.logical_not(early))
    def _():
        send()

    at = lax.broadcasted_iota(jnp.int32, perm.shape, 0)
    taken = jnp.where(at < LANES, 2 * at, 2 * at - 2 * LANES + 1)
    perm[...] = (taken == lax.broadcasted_iota(jnp.int32, perm.shape, 1)).astype(jnp.float32).astype(jnp.bfloat16)
    for load in loads:
        load.wait()
    base = jnp.maximum(chip - 1, 0) * 2
    block = chip * 2 + core - base

    shape = (LANES * heads, LANES)
    row = lax.broadcasted_iota(jnp.int32, shape, 0)
    first_half = lax.rem(row, heads) < heads // 2
    for tile in range(rows // LANES):
        span = pl.ds(tile * LANES * heads, LANES * heads)
        q = q_in[span, :].astype(jnp.float32)
        q_aug[span, 0:width] = jnp.where(first_half, q, 0.0).astype(jnp.bfloat16)
        q_aug[span, width:2 * width] = jnp.where(first_half, 0.0, q).astype(jnp.bfloat16)
        ids = seg[pl.ds(block * 4 + tile, 1), :].astype(jnp.float32)
        picked = jnp.where(row // heads == lax.broadcasted_iota(jnp.int32, shape, 1), ids, 0.0)
        seg_q[span, :] = jnp.dot(
            picked.astype(jnp.bfloat16), jnp.ones((LANES, LANES), jnp.bfloat16), preferred_element_type=jnp.float32)

    def process(kv_ref, key_block, tiles, first_token, last_token, own_keys=False, init=False, recv=None, last=False):
        if recv is not None:
            for tile in tiles:
                for kv in range(2):
                    wait_for(kv_ref, recv, tile, kv)
            recv = None

        def parted(kv, tile):
            if recv is not None:
                wait_for(kv_ref, recv, tile, kv)
            return jnp.dot(
                perm[...], kv_ref[kv, pl.ds(tile * kv_rows, kv_rows), :], preferred_element_type=jnp.float32)

        for part, tile in enumerate(tiles):
            span = pl.ds(part * LANES, LANES)
            both = parted(0, tile)
            k_t[0:width, span] = both[:LANES].T.astype(jnp.bfloat16)
            k_t[width:2 * width, span] = both[LANES:].T.astype(jnp.bfloat16)
        ids = jnp.concatenate(
            [seg[pl.ds(key_block * 4 + tile, 1), :] for tile in tiles], axis=1).astype(jnp.float32)

        begin, count = first_token * heads, (last_token - first_token) * heads
        span = pl.ds(begin, count)
        scores = jnp.dot(q_aug[span, :], k_t[...], preferred_element_type=jnp.float32)
        allowed = jnp.concatenate([seg_q[span, :]] * len(tiles), axis=1) == ids
        if own_keys:
            line = lax.broadcasted_iota(jnp.int32, scores.shape, 0)
            key = lax.broadcasted_iota(jnp.int32, scores.shape, 1)
            allowed = allowed & (line - heads * key >= heads * tiles[0] * LANES - begin)
        scores = jnp.where(allowed, scores, BIG)
        peak = jnp.max(scores, axis=1, keepdims=True)
        if init:
            new_top = jnp.broadcast_to(peak, (count, LANES))
        else:
            old_top = top[span, :]
            new_top = jnp.maximum(old_top, peak)
        weights = jnp.exp2((scores - jnp.concatenate([new_top] * len(tiles), axis=1)) * c)
        added = weights[:, :LANES] + weights[:, LANES:]
        weights = weights.astype(jnp.bfloat16)
        for part, tile in enumerate(tiles):
            both = parted(1, tile)
            v_cat[pl.ds(part * LANES, LANES), 0:width] = both[:LANES].astype(jnp.bfloat16)
            v_cat[pl.ds(part * LANES, LANES), width:2 * width] = both[LANES:].astype(jnp.bfloat16)
        mixed = jnp.dot(weights, v_cat[...], preferred_element_type=jnp.float32)
        line = lax.broadcasted_iota(jnp.int32, (count, width), 0)
        mixed = jnp.where(lax.rem(line, heads) < heads // 2, mixed[:, :width], mixed[:, width:])
        if not init:
            fade = jnp.exp2((old_top - new_top) * c)
            added = total[span, :] * fade + added
            mixed = acc[span, :] * fade + mixed
        if last:
            out[span, :] = (mixed / jnp.sum(added, axis=1, keepdims=True)).astype(jnp.bfloat16)
        else:
            top[span, :] = new_top
            total[span, :] = added
            acc[span, :] = mixed

    def finish(first_token, last_token):
        span = pl.ds(first_token * heads, (last_token - first_token) * heads)
        out[span, :] = (acc[span, :] / jnp.sum(total[span, :], axis=1, keepdims=True)).astype(jnp.bfloat16)

    half = rows // 2
    process(own, block, (0, 1), 0, rows, own_keys=True, init=True)
    process(own, block, (2, 3), half, rows, own_keys=True)

    @pl.when(early)
    def _():
        send()

    @pl.when(core == 1)
    def _():
        for tiles in ((1, 3), (0, 2)):
            process(near, block - 1, tiles, 0, rows, recv=recv_near if tiles[0] == 0 else None)

    @pl.when(has_before & (core == 0))
    def _():
        for direct, passed in ((1, 3), (0, 2)):
            wait_recv(second_by_0(direct))
            start(pass_to_1(direct))
            wait_recv(pass_to_0(passed))
            process(near, block - 1, (direct, passed), 0, rows)

    @pl.when(has_before & (core == 1))
    def _():
        for tile in (3, 2):
            wait_recv(second_by_1(tile))
            start(pass_to_0(tile))
        process(far, block - 2, (2, 3), 0, rows)

    @pl.when(has_before & (core == 0))
    def _():
        process(far, block - 2, (2, 3), 0, rows, recv=recv_far)

    finish(half, rows)

    @pl.when(has_before)
    def _():
        process(far, block - 2, (0, 1), 0, half, recv=recv_far, last=True)

    @pl.when(jnp.logical_not(has_before))
    def _():
        finish(0, half)

    @pl.when(has_after & (core == 1))
    def _():
        for pair in (second_by_1(3), second_by_1(2), to_relay(1), to_relay(0), first_by_1(3), first_by_1(1)):
            wait_send(pair)

    @pl.when(has_before & (core == 1))
    def _():
        for pair in (pass_to_0(3), pass_to_0(2)):
            wait_send(pair)

    @pl.when(core == 0)
    def _():
        for tile in (3, 1, 2, 0):
            wait_send(to_core_1(tile))

    @pl.when(has_after & (core == 0))
    def _():
        for pair in (second_by_0(1), second_by_0(0), first_by_0(2), first_by_0(0)):
            wait_send(pair)

    @pl.when(has_before & (core == 0))
    def _():
        for pair in (pass_to_1(1), pass_to_1(0)):
            wait_send(pair)


def shards(queries, keys, values, segment_ids):
    rows, heads, width = queries.shape
    kv_heads = keys.shape[1]
    dims = (lax.axis_size("inner"), lax.axis_size("outer"), rows, width)
    in_hbm = pl.BlockSpec(memory_space=pltpu.HBM)
    kv = lambda parts=1: pltpu.VMEM((2, rows * kv_heads // parts, width), jnp.bfloat16)
    wide = lambda: pltpu.VMEM((rows * heads, width), jnp.float32)
    sems = lambda count: pltpu.SemaphoreType.DMA((count, 2))
    result = pl.pallas_call(
        functools.partial(kernel, dims),
        out_shape=pltpu.VMEM((rows * heads, width), jnp.bfloat16),
        in_specs=[in_hbm] * 4,
        out_specs=pl.BlockSpec(memory_space=pltpu.VMEM),
        scratch_shapes=[
            pltpu.VMEM((rows * heads, width), jnp.bfloat16),
            pltpu.VMEM((rows * heads, 2 * width), jnp.bfloat16),
            kv(), kv(), kv(), kv(2),
            pltpu.VMEM((16, LANES), jnp.int32),
            wide(),
            pltpu.VMEM((2 * LANES, 2 * LANES), jnp.bfloat16),
            pltpu.VMEM((2 * width, 2 * LANES), jnp.bfloat16),
            pltpu.VMEM((2 * LANES, 2 * width), jnp.bfloat16),
            wide(), wide(), wide(),
            pltpu.SemaphoreType.DMA((4,)),
            sems(8), sems(4), sems(4), sems(4), sems(2), sems(2),
        ],
        compiler_params=pltpu.CompilerParams(
            collective_id=0, has_side_effects=True, vmem_limit_bytes=48 * 1024 * 1024),
    )(*[pltpu.with_memory_space_constraint(operand, pltpu.HBM) for operand in (
        queries.reshape(rows * heads, width),
        keys.reshape(rows * kv_heads, width),
        values.reshape(rows * kv_heads, width),
        segment_ids.reshape(-1, LANES),
    )])
    return result.reshape(rows, heads, width)


def solution(mesh):
    return jax.shard_map(
        shards,
        mesh=mesh,
        in_specs=(
            P(("outer", "inner"), "head", None),
            P(("outer", "inner"), "head", None),
            P(("outer", "inner"), "head", None),
            P(),
        ),
        out_specs=P(("outer", "inner"), "head", None),
        check_vma=False,
    )
```

```python
import functools

import jax
import jax.numpy as jnp
from jax import lax
from jax.experimental import pallas as pl
from jax.experimental.pallas import tpu as pltpu
from jax.sharding import PartitionSpec as P

MESH = pl.DeviceIdType.MESH
BIG = -1e30
LOG2E = 1.4426950408889634
LANES = 128


def kernel(dims, q_hbm, k_hbm, v_hbm, s_hbm, out, q_in, q_aug, own, near, far, relay, seg, seg_q,
           perm, k_t, v_cat, top, total, acc, in_sem,
           send_sem, pass_sem, recv_near, recv_far, relay_send, relay_recv):
    inner_size, outer_size, rows, width = dims
    chips_in = inner_size // 2
    outer, inner, head = lax.axis_index("outer"), lax.axis_index("inner"), lax.axis_index("head")
    chip, core = outer * chips_in + inner // 2, lax.rem(inner, 2)
    early = lax.rem(chip, 2) == 0
    has_before, has_after = chip > 0, chip < outer_size * chips_in - 1
    heads = q_in.shape[0] // rows
    kv_rows = own.shape[1] // rows * LANES
    c = (width ** -0.5) * LOG2E

    def device(index, which):
        return (index // chips_in, lax.rem(index, chips_in) * 2 + which, head)

    sibling = (outer, inner + 1 - 2 * core, head)

    barrier = pltpu.get_barrier_semaphore()
    pl.semaphore_signal(barrier, inc=1, device_id=sibling, device_id_type=MESH)

    @pl.when(has_before)
    def _():
        pl.semaphore_signal(barrier, inc=1, device_id=device(chip - 1, 1), device_id_type=MESH)

    @pl.when(has_before & (core == 0))
    def _():
        pl.semaphore_signal(barrier, inc=1, device_id=device(chip - 1, 0), device_id_type=MESH)

    loads = [
        pltpu.make_async_copy(k_hbm, own.at[0], in_sem.at[0]),
        pltpu.make_async_copy(v_hbm, own.at[1], in_sem.at[1]),
        pltpu.make_async_copy(q_hbm, q_in, in_sem.at[2]),
        pltpu.make_async_copy(s_hbm.at[pl.ds(pl.multiple_of(jnp.maximum(chip - 1, 0) * 8, 8), 16)], seg, in_sem.at[3]),
    ]

    def piece(ref, tile):
        return ref.at[pl.ds(tile * kv_rows, kv_rows)]

    def copy_of(source, target, tile, kv, send, recv, to, slot=0):
        return pltpu.make_async_remote_copy(
            src_ref=piece(source, tile), dst_ref=piece(target.at[kv], tile),
            send_sem=send.at[slot + tile, kv], recv_sem=recv.at[tile, kv], device_id=to, device_id_type=MESH)

    def second_keys(tile):
        return copy_of(k_hbm, far, tile, 0, send_sem, recv_far, device(chip + 1, 1))

    def first_keys(tile):
        return copy_of(near.at[0], far, tile, 0, send_sem, recv_far, device(chip + 1, 0), 4)

    def second_values(tile):
        return copy_of(relay, near, tile, 1, send_sem, recv_near, device(chip + 1, 0))

    def first_values(tile):
        return copy_of(v_hbm, far, tile, 1, send_sem, recv_far, device(chip + 1, 0), 4)

    def to_core_1(tile, kv):
        return copy_of((k_hbm, v_hbm)[kv], near, tile, kv, pass_sem, recv_near, sibling)

    def to_relay(tile):
        return pltpu.make_async_remote_copy(
            src_ref=piece(v_hbm, tile), dst_ref=piece(relay, tile), send_sem=relay_send.at[tile],
            recv_sem=relay_recv.at[tile], device_id=sibling, device_id_type=MESH)

    def pass_keys(tile):
        return copy_of(far.at[0], near, tile, 0, pass_sem, recv_near, sibling)

    def pass_values(tile):
        return copy_of(near.at[1], far, tile, 1, pass_sem, recv_far, sibling, 4)

    def wait_near(tile, kv):
        to_core_1(tile, kv).wait_recv()

    def wait_far(tile, kv):
        copy_of((k_hbm, v_hbm)[kv], far, tile, kv, pass_sem, recv_far, sibling).wait_recv()

    order = (3, 2, 1, 0)

    def send():
        pl.semaphore_wait(barrier, 1 + has_after.astype(jnp.int32) * (1 + core))

        @pl.when(core == 1)
        def _():
            @pl.when(has_after)
            def _():
                for tile in order:
                    to_relay(tile).start()
                    second_keys(tile).start()
            for tile in order:
                wait_near(tile, 0)

            @pl.when(has_after)
            def _():
                for tile in order:
                    first_keys(tile).start()

        @pl.when(core == 0)
        def _():
            for kv in range(2):
                for tile in order:
                    to_core_1(tile, kv).start()

            @pl.when(has_after)
            def _():
                for tile in order:
                    to_relay(tile).wait_recv()
                    second_values(tile).start()
                for tile in order:
                    first_values(tile).start()

    for load in loads:
        load.start()

    @pl.when(jnp.logical_not(early))
    def _():
        send()

    at = lax.broadcasted_iota(jnp.int32, perm.shape, 0)
    taken = jnp.where(at < LANES, 2 * at, 2 * at - 2 * LANES + 1)
    perm[...] = (taken == lax.broadcasted_iota(jnp.int32, perm.shape, 1)).astype(jnp.float32).astype(jnp.bfloat16)
    for load in loads:
        load.wait()
    base = jnp.maximum(chip - 1, 0) * 2
    block = chip * 2 + core - base

    shape = (LANES * heads, LANES)
    row = lax.broadcasted_iota(jnp.int32, shape, 0)
    first_half = lax.rem(row, heads) < heads // 2
    for tile in range(rows // LANES):
        span = pl.ds(tile * LANES * heads, LANES * heads)
        q = q_in[span, :].astype(jnp.float32)
        q_aug[span, 0:width] = jnp.where(first_half, q, 0.0).astype(jnp.bfloat16)
        q_aug[span, width:2 * width] = jnp.where(first_half, 0.0, q).astype(jnp.bfloat16)
        ids = seg[pl.ds(block * 4 + tile, 1), :].astype(jnp.float32)
        picked = jnp.where(row // heads == lax.broadcasted_iota(jnp.int32, shape, 1), ids, 0.0)
        seg_q[span, :] = jnp.dot(
            picked.astype(jnp.bfloat16), jnp.ones((LANES, LANES), jnp.bfloat16), preferred_element_type=jnp.float32)

    def process(kv_ref, key_block, tiles, spans, own_keys=False, init=False, last=False):
        for part, tile in enumerate(tiles):
            span = pl.ds(part * LANES, LANES)
            parted = [
                jnp.dot(perm[...], kv_ref[kv, pl.ds(tile * kv_rows, kv_rows), :], preferred_element_type=jnp.float32)
                for kv in range(2)]
            k_t[0:width, span] = parted[0][:LANES].T.astype(jnp.bfloat16)
            k_t[width:2 * width, span] = parted[0][LANES:].T.astype(jnp.bfloat16)
            v_cat[span, 0:width] = parted[1][:LANES].astype(jnp.bfloat16)
            v_cat[span, width:2 * width] = parted[1][LANES:].astype(jnp.bfloat16)
        for first_token, last_token, low in spans:
            step(key_block, tiles[low:], slice(low * LANES, len(tiles) * LANES), first_token, last_token,
                 own_keys, init, last)

    def step(key_block, tiles, reach, first_token, last_token, own_keys, init, last):
        ids = jnp.concatenate(
            [seg[pl.ds(key_block * 4 + tile, 1), :] for tile in tiles], axis=1).astype(jnp.float32)
        begin, count = first_token * heads, (last_token - first_token) * heads
        span = pl.ds(begin, count)
        scores = jnp.dot(q_aug[span, :], k_t[:, reach], preferred_element_type=jnp.float32)
        allowed = jnp.concatenate([seg_q[span, :]] * len(tiles), axis=1) == ids
        if own_keys:
            line = lax.broadcasted_iota(jnp.int32, scores.shape, 0)
            key = lax.broadcasted_iota(jnp.int32, scores.shape, 1)
            allowed = allowed & (line - heads * key >= heads * tiles[0] * LANES - begin)
        scores = jnp.where(allowed, scores, BIG)
        peak = jnp.max(scores, axis=1, keepdims=True)
        if init:
            new_top = jnp.broadcast_to(peak, (count, LANES))
        else:
            old_top = top[span, :]
            new_top = jnp.maximum(old_top, peak)
        weights = jnp.exp2((scores - jnp.concatenate([new_top] * len(tiles), axis=1)) * c)
        added = weights if len(tiles) == 1 else weights[:, :LANES] + weights[:, LANES:]
        mixed = jnp.dot(weights.astype(jnp.bfloat16), v_cat[reach, :], preferred_element_type=jnp.float32)
        line = lax.broadcasted_iota(jnp.int32, (count, width), 0)
        mixed = jnp.where(lax.rem(line, heads) < heads // 2, mixed[:, :width], mixed[:, width:])
        if not init:
            fade = jnp.exp2((old_top - new_top) * c)
            added = total[span, :] * fade + added
            mixed = acc[span, :] * fade + mixed
        if last:
            out[span, :] = (mixed / jnp.sum(added, axis=1, keepdims=True)).astype(jnp.bfloat16)
        else:
            top[span, :] = new_top
            total[span, :] = added
            acc[span, :] = mixed

    def finish(first_token, last_token):
        span = pl.ds(first_token * heads, (last_token - first_token) * heads)
        out[span, :] = (acc[span, :] / jnp.sum(total[span, :], axis=1, keepdims=True)).astype(jnp.bfloat16)

    half = rows // 2
    process(own, block, (0, 1), [(0, rows, 0)], own_keys=True, init=True)
    process(own, block, (2, 3), [(half, rows, 0)], own_keys=True)

    @pl.when(early)
    def _():
        send()

    for tiles in ((2, 3), (0, 1)):
        @pl.when(core == 1)
        def _():
            for tile in tiles:
                wait_near(tile, 1)

        @pl.when(has_before & (core == 0))
        def _():
            for tile in reversed(tiles):
                wait_near(tile, 1)
                pass_values(tile).start()
            for tile in tiles:
                wait_near(tile, 0)

        @pl.when(has_before | (core == 1))
        def _():
            process(near, block - 1, tiles, [(0, rows, 0)])

    @pl.when(has_before & (core == 1))
    def _():
        for tile in order:
            wait_far(tile, 0)
            pass_keys(tile).start()

    def far_step(tiles, spans, last=False):
        @pl.when(has_before & (core == 0))
        def _():
            for tile in tiles:
                wait_far(tile, 0)

        @pl.when(has_before)
        def _():
            for tile in tiles:
                wait_far(tile, 1)
            process(far, block - 2, tiles, spans, last=last)

    far_step((2, 3), [(0, rows - LANES, 0), (rows - LANES, rows, 1)])
    finish(half, rows)
    @pl.when(core == 0)
    def _():
        for tile in order:
            for kv in range(2):
                to_core_1(tile, kv).wait_send()

    @pl.when(has_before & (core == 0))
    def _():
        for tile in order:
            pass_values(tile).wait_send()

    far_step((0, 1), [(0, LANES, 0), (LANES, half, 1)], last=True)

    @pl.when(jnp.logical_not(has_before))
    def _():
        finish(0, half)

    @pl.when(has_after & (core == 1))
    def _():
        for tile in order:
            to_relay(tile).wait_send()
            second_keys(tile).wait_send()
            first_keys(tile).wait_send()

    @pl.when(has_after & (core == 0))
    def _():
        for tile in order:
            second_values(tile).wait_send()
            first_values(tile).wait_send()

    @pl.when(has_before & (core == 1))
    def _():
        for tile in order:
            pass_keys(tile).wait_send()


def shards(queries, keys, values, segment_ids):
    rows, heads, width = queries.shape
    kv_heads = keys.shape[1]
    dims = (lax.axis_size("inner"), lax.axis_size("outer"), rows, width)
    in_hbm = pl.BlockSpec(memory_space=pltpu.HBM)
    kv = lambda: pltpu.VMEM((2, rows * kv_heads, width), jnp.bfloat16)
    wide = lambda: pltpu.VMEM((rows * heads, width), jnp.float32)
    sems = lambda count: pltpu.SemaphoreType.DMA((count, 2))
    result = pl.pallas_call(
        functools.partial(kernel, dims),
        out_shape=pltpu.VMEM((rows * heads, width), jnp.bfloat16),
        in_specs=[in_hbm] * 4,
        out_specs=pl.BlockSpec(memory_space=pltpu.VMEM),
        scratch_shapes=[
            pltpu.VMEM((rows * heads, width), jnp.bfloat16),
            pltpu.VMEM((rows * heads, 2 * width), jnp.bfloat16),
            kv(), kv(), kv(),
            pltpu.VMEM((rows * kv_heads, width), jnp.bfloat16),
            pltpu.VMEM((16, LANES), jnp.int32),
            wide(),
            pltpu.VMEM((2 * LANES, 2 * LANES), jnp.bfloat16),
            pltpu.VMEM((2 * width, 2 * LANES), jnp.bfloat16),
            pltpu.VMEM((2 * LANES, 2 * width), jnp.bfloat16),
            wide(), wide(), wide(),
            pltpu.SemaphoreType.DMA((4,)),
            sems(8), sems(8), sems(4), sems(4),
            pltpu.SemaphoreType.DMA((4,)),
            pltpu.SemaphoreType.DMA((4,)),
        ],
        compiler_params=pltpu.CompilerParams(
            collective_id=0, has_side_effects=True, vmem_limit_bytes=48 * 1024 * 1024),
    )(*[pltpu.with_memory_space_constraint(operand, pltpu.HBM) for operand in (
        queries.reshape(rows * heads, width),
        keys.reshape(rows * kv_heads, width),
        values.reshape(rows * kv_heads, width),
        segment_ids.reshape(-1, LANES),
    )])
    return result.reshape(rows, heads, width)


def solution(mesh):
    return jax.shard_map(
        shards,
        mesh=mesh,
        in_specs=(
            P(("outer", "inner"), "head", None),
            P(("outer", "inner"), "head", None),
            P(("outer", "inner"), "head", None),
            P(),
        ),
        out_specs=P(("outer", "inner"), "head", None),
        check_vma=False,
    )
```

```python
import functools

import jax
import jax.numpy as jnp
from jax import lax
from jax.experimental import pallas as pl
from jax.experimental.pallas import tpu as pltpu
from jax.sharding import PartitionSpec as P

MESH = pl.DeviceIdType.MESH
BIG = -1e30
LOG2E = 1.4426950408889634
LANES = 128


def kernel(dims, q_hbm, k_hbm, v_hbm, s_hbm, out, q_in, q_aug, own, near, far, relay, seg, seg_q,
           perm, k_t, v_cat, top, total, acc, in_sem,
           send_sem, pass_sem, recv_near, recv_far, relay_send, relay_recv):
    inner_size, outer_size, rows, width = dims
    chips_in = inner_size // 2
    outer, inner, head = lax.axis_index("outer"), lax.axis_index("inner"), lax.axis_index("head")
    chip, core = outer * chips_in + inner // 2, lax.rem(inner, 2)
    early = lax.rem(chip, 2) == 0
    has_before, has_after = chip > 0, chip < outer_size * chips_in - 1
    heads = q_in.shape[0] // rows
    kv_rows = own.shape[1] // rows * LANES
    c = (width ** -0.5) * LOG2E

    def device(index, which):
        return (index // chips_in, lax.rem(index, chips_in) * 2 + which, head)

    sibling = (outer, inner + 1 - 2 * core, head)

    barrier = pltpu.get_barrier_semaphore()
    pl.semaphore_signal(barrier, inc=1, device_id=sibling, device_id_type=MESH)

    @pl.when(has_before)
    def _():
        pl.semaphore_signal(barrier, inc=1, device_id=device(chip - 1, 1), device_id_type=MESH)

    @pl.when(has_before & (core == 0))
    def _():
        pl.semaphore_signal(barrier, inc=1, device_id=device(chip - 1, 0), device_id_type=MESH)

    loads = [
        pltpu.make_async_copy(k_hbm, own.at[0], in_sem.at[0]),
        pltpu.make_async_copy(v_hbm, own.at[1], in_sem.at[1]),
        pltpu.make_async_copy(q_hbm, q_in, in_sem.at[2]),
        pltpu.make_async_copy(s_hbm.at[pl.ds(pl.multiple_of(jnp.maximum(chip - 1, 0) * 8, 8), 16)], seg, in_sem.at[3]),
    ]

    def piece(ref, tile):
        return ref.at[pl.ds(tile * kv_rows, kv_rows)]

    def copy_of(source, target, tile, kv, send, recv, to, slot=0):
        return pltpu.make_async_remote_copy(
            src_ref=piece(source, tile), dst_ref=piece(target.at[kv], tile),
            send_sem=send.at[slot + tile, kv], recv_sem=recv.at[tile, kv], device_id=to, device_id_type=MESH)

    def second_keys(tile):
        return copy_of(k_hbm, far, tile, 0, send_sem, recv_far, device(chip + 1, 1))

    def first_keys(tile):
        return copy_of(near.at[0], far, tile, 0, send_sem, recv_far, device(chip + 1, 0), 4)

    def second_values(tile):
        return copy_of(relay, near, tile, 1, send_sem, recv_near, device(chip + 1, 0))

    def first_values(tile):
        return copy_of(v_hbm, far, tile, 1, send_sem, recv_far, device(chip + 1, 0), 4)

    def to_core_1(tile, kv):
        return copy_of((k_hbm, v_hbm)[kv], near, tile, kv, pass_sem, recv_near, sibling)

    def to_relay(tile):
        return pltpu.make_async_remote_copy(
            src_ref=piece(v_hbm, tile), dst_ref=piece(relay, tile), send_sem=relay_send.at[tile],
            recv_sem=relay_recv.at[tile], device_id=sibling, device_id_type=MESH)

    def pass_keys(tile):
        return copy_of(far.at[0], near, tile, 0, pass_sem, recv_near, sibling)

    def pass_values(tile):
        return copy_of(near.at[1], far, tile, 1, pass_sem, recv_far, sibling, 4)

    def wait_near(tile, kv):
        to_core_1(tile, kv).wait_recv()

    def wait_far(tile, kv):
        copy_of((k_hbm, v_hbm)[kv], far, tile, kv, pass_sem, recv_far, sibling).wait_recv()

    order = (3, 2, 1, 0)

    def send():
        pl.semaphore_wait(barrier, 1 + has_after.astype(jnp.int32) * (1 + core))

        @pl.when(core == 1)
        def _():
            @pl.when(has_after)
            def _():
                for tile in order:
                    to_relay(tile).start()
                    second_keys(tile).start()
            for tile in order:
                wait_near(tile, 0)

            @pl.when(has_after)
            def _():
                for tile in order:
                    first_keys(tile).start()

        @pl.when(core == 0)
        def _():
            for kv in range(2):
                for tile in order:
                    to_core_1(tile, kv).start()

            @pl.when(has_after)
            def _():
                for tile in order:
                    to_relay(tile).wait_recv()
                    second_values(tile).start()
                for tile in order:
                    first_values(tile).start()

    for load in loads:
        load.start()

    @pl.when(jnp.logical_not(early))
    def _():
        send()

    at = lax.broadcasted_iota(jnp.int32, perm.shape, 0)
    taken = jnp.where(at < LANES, 2 * at, 2 * at - 2 * LANES + 1)
    perm[...] = (taken == lax.broadcasted_iota(jnp.int32, perm.shape, 1)).astype(jnp.float32).astype(jnp.bfloat16)
    for load in loads:
        load.wait()
    base = jnp.maximum(chip - 1, 0) * 2
    block = chip * 2 + core - base

    shape = (LANES * heads, LANES)
    row = lax.broadcasted_iota(jnp.int32, shape, 0)
    first_half = lax.rem(row, heads) < heads // 2
    for tile in range(rows // LANES):
        span = pl.ds(tile * LANES * heads, LANES * heads)
        q = q_in[span, :].astype(jnp.float32)
        q_aug[span, 0:width] = jnp.where(first_half, q, 0.0).astype(jnp.bfloat16)
        q_aug[span, width:2 * width] = jnp.where(first_half, 0.0, q).astype(jnp.bfloat16)
        ids = seg[pl.ds(block * 4 + tile, 1), :].astype(jnp.float32)
        picked = jnp.where(row // heads == lax.broadcasted_iota(jnp.int32, shape, 1), ids, 0.0)
        seg_q[span, :] = jnp.dot(
            picked.astype(jnp.bfloat16), jnp.ones((LANES, LANES), jnp.bfloat16), preferred_element_type=jnp.float32)

    def process(kv_ref, key_block, tiles, spans, own_keys=False, init=False, last=1 << 30):
        for part, tile in enumerate(tiles):
            span = pl.ds(part * LANES, LANES)
            parted = [
                jnp.dot(perm[...], kv_ref[kv, pl.ds(tile * kv_rows, kv_rows), :], preferred_element_type=jnp.float32)
                for kv in range(2)]
            k_t[0:width, span] = parted[0][:LANES].T.astype(jnp.bfloat16)
            k_t[width:2 * width, span] = parted[0][LANES:].T.astype(jnp.bfloat16)
            v_cat[span, 0:width] = parted[1][:LANES].astype(jnp.bfloat16)
            v_cat[span, width:2 * width] = parted[1][LANES:].astype(jnp.bfloat16)
        for first_token, last_token, low in spans:
            step(key_block, tiles[low:], slice(low * LANES, len(tiles) * LANES), first_token, last_token,
                 own_keys, init, first_token >= last)

    def step(key_block, tiles, reach, first_token, last_token, own_keys, init, last):
        ids = jnp.concatenate(
            [seg[pl.ds(key_block * 4 + tile, 1), :] for tile in tiles], axis=1).astype(jnp.float32)
        begin, count = first_token * heads, (last_token - first_token) * heads
        span = pl.ds(begin, count)
        scores = jnp.dot(q_aug[span, :], k_t[:, reach], preferred_element_type=jnp.float32)
        allowed = jnp.concatenate([seg_q[span, :]] * len(tiles), axis=1) == ids
        if own_keys:
            line = lax.broadcasted_iota(jnp.int32, scores.shape, 0)
            key = lax.broadcasted_iota(jnp.int32, scores.shape, 1)
            allowed = allowed & (line - heads * key >= heads * tiles[0] * LANES - begin)
        scores = jnp.where(allowed, scores, BIG)
        peak = jnp.max(scores, axis=1, keepdims=True)
        if init:
            new_top = jnp.broadcast_to(peak, (count, LANES))
        else:
            old_top = top[span, :]
            new_top = jnp.maximum(old_top, peak)
        weights = jnp.exp2((scores - jnp.concatenate([new_top] * len(tiles), axis=1)) * c)
        added = weights if len(tiles) == 1 else weights[:, :LANES] + weights[:, LANES:]
        mixed = jnp.dot(weights.astype(jnp.bfloat16), v_cat[reach, :], preferred_element_type=jnp.float32)
        line = lax.broadcasted_iota(jnp.int32, (count, width), 0)
        mixed = jnp.where(lax.rem(line, heads) < heads // 2, mixed[:, :width], mixed[:, width:])
        if not init:
            fade = jnp.exp2((old_top - new_top) * c)
            added = total[span, :] * fade + added
            mixed = acc[span, :] * fade + mixed
        if last:
            out[span, :] = (mixed / jnp.sum(added, axis=1, keepdims=True)).astype(jnp.bfloat16)
        else:
            top[span, :] = new_top
            total[span, :] = added
            acc[span, :] = mixed

    def finish(first_token, last_token):
        span = pl.ds(first_token * heads, (last_token - first_token) * heads)
        out[span, :] = (acc[span, :] / jnp.sum(total[span, :], axis=1, keepdims=True)).astype(jnp.bfloat16)

    half = rows // 2
    process(own, block, (0, 1), [(0, rows, 0)], own_keys=True, init=True)
    process(own, block, (2, 3), [(half, rows, 0)], own_keys=True)

    @pl.when(early)
    def _():
        send()

    for tiles in ((2, 3), (0, 1)):
        @pl.when(core == 1)
        def _():
            for tile in tiles:
                wait_near(tile, 1)

        @pl.when(has_before & (core == 0))
        def _():
            for tile in reversed(tiles):
                wait_near(tile, 1)
                pass_values(tile).start()
            for tile in tiles:
                wait_near(tile, 0)

        @pl.when(has_before | (core == 1))
        def _():
            process(near, block - 1, tiles, [(0, rows, 0)])

    @pl.when(has_before & (core == 1))
    def _():
        for tile in order:
            wait_far(tile, 0)
            pass_keys(tile).start()

    def far_step(tiles, spans, last):
        @pl.when(has_before & (core == 0))
        def _():
            for tile in tiles:
                wait_far(tile, 0)

        @pl.when(has_before)
        def _():
            for tile in tiles:
                wait_far(tile, 1)
            process(far, block - 2, tiles, spans, last=last)

    far_step((2, 3), [(0, half, 0), (half, rows - LANES, 0), (rows - LANES, rows, 1)], last=half)
    @pl.when(core == 0)
    def _():
        for tile in order:
            for kv in range(2):
                to_core_1(tile, kv).wait_send()

    @pl.when(has_before & (core == 0))
    def _():
        for tile in order:
            pass_values(tile).wait_send()

    far_step((0, 1), [(0, LANES, 0), (LANES, half, 1)], last=0)

    @pl.when(jnp.logical_not(has_before))
    def _():
        finish(0, rows)

    @pl.when(has_after & (core == 1))
    def _():
        for tile in order:
            to_relay(tile).wait_send()
            second_keys(tile).wait_send()
            first_keys(tile).wait_send()

    @pl.when(has_after & (core == 0))
    def _():
        for tile in order:
            second_values(tile).wait_send()
            first_values(tile).wait_send()

    @pl.when(has_before & (core == 1))
    def _():
        for tile in order:
            pass_keys(tile).wait_send()


def shards(queries, keys, values, segment_ids):
    rows, heads, width = queries.shape
    kv_heads = keys.shape[1]
    dims = (lax.axis_size("inner"), lax.axis_size("outer"), rows, width)
    in_hbm = pl.BlockSpec(memory_space=pltpu.HBM)
    kv = lambda: pltpu.VMEM((2, rows * kv_heads, width), jnp.bfloat16)
    wide = lambda: pltpu.VMEM((rows * heads, width), jnp.float32)
    sems = lambda count: pltpu.SemaphoreType.DMA((count, 2))
    result = pl.pallas_call(
        functools.partial(kernel, dims),
        out_shape=pltpu.VMEM((rows * heads, width), jnp.bfloat16),
        in_specs=[in_hbm] * 4,
        out_specs=pl.BlockSpec(memory_space=pltpu.VMEM),
        scratch_shapes=[
            pltpu.VMEM((rows * heads, width), jnp.bfloat16),
            pltpu.VMEM((rows * heads, 2 * width), jnp.bfloat16),
            kv(), kv(), kv(),
            pltpu.VMEM((rows * kv_heads, width), jnp.bfloat16),
            pltpu.VMEM((16, LANES), jnp.int32),
            wide(),
            pltpu.VMEM((2 * LANES, 2 * LANES), jnp.bfloat16),
            pltpu.VMEM((2 * width, 2 * LANES), jnp.bfloat16),
            pltpu.VMEM((2 * LANES, 2 * width), jnp.bfloat16),
            wide(), wide(), wide(),
            pltpu.SemaphoreType.DMA((4,)),
            sems(8), sems(8), sems(4), sems(4),
            pltpu.SemaphoreType.DMA((4,)),
            pltpu.SemaphoreType.DMA((4,)),
        ],
        compiler_params=pltpu.CompilerParams(
            collective_id=0, has_side_effects=True, vmem_limit_bytes=48 * 1024 * 1024),
    )(*[pltpu.with_memory_space_constraint(operand, pltpu.HBM) for operand in (
        queries.reshape(rows * heads, width),
        keys.reshape(rows * kv_heads, width),
        values.reshape(rows * kv_heads, width),
        segment_ids.reshape(-1, LANES),
    )])
    return result.reshape(rows, heads, width)


def solution(mesh):
    return jax.shard_map(
        shards,
        mesh=mesh,
        in_specs=(
            P(("outer", "inner"), "head", None),
            P(("outer", "inner"), "head", None),
            P(("outer", "inner"), "head", None),
            P(),
        ),
        out_specs=P(("outer", "inner"), "head", None),
        check_vma=False,
    )
```
